256 devices in a mesh: dp: 8 (over z_lo, x), tensor: 32 (over y, z_hi, core).
Axes of the slice: x: 4, y: 4, z: 8 (z_hi: 4, z_lo: 2; z = z_hi * 2 + z_lo), core: 2. Of those that a mesh axis runs over, the one named last changes fastest.
Arguments:
- activations: bfloat16 [24, 256, 16384], P('dp', None, 'tensor'), may hold values from -6 to 6
- out_grads: bfloat16 [24, 256, 8192], P('dp', 'tensor'), may hold values from -0.5 to 0.5
Outputs:
- fisher: float32 [8192, 16384], P('dp', 'tensor')
The draws below stay inside these ranges and needn't reach their ends.
All inputs are finite; a program needn't handle non-finite values.
Results may differ from the reference program's by a relative error of at most 0.0003.
Values may be sent and summed in bfloat16 or wider, within the bound.
No kernel may reach another device: no remote copies, remote signals or barrier semaphores. Data moves between devices by JAX's collectives and lax.ppermute only.
A program may use at most 128 MiB of HBM per device.

```python
import jax
import jax.numpy as jnp
from jax import lax

D = 8192
FF = 16384
L = 256
SEQS = 24


def strengthened(array, stream_key, source, target, parts, factor):
    owner, partner = [(jnp.arange(array.shape[axis_at]) // (array.shape[axis_at] // parts)).reshape([-1 if axis == axis_at else 1 for axis in range(array.ndim)]) for axis_at in (source, target)]
    chosen = jax.random.permutation(stream_key, parts)[partner]
    strong = (owner == chosen) | (owner == (partner + parts // 2) % parts)
    return jnp.where(strong, factor * array, array)


def steps_of(key, dims, shards, least, largest):
    def one(position, parts):
        draws = jax.random.uniform(jax.random.fold_in(jax.random.fold_in(key, 6), position), (parts,), jnp.float32, least / len(shards), largest / len(shards))
        return jnp.repeat(jnp.exp(draws), dims[position] // parts).reshape((-1,) + (1,) * (len(dims) - position - 1))

    factor_of = one(*shards[0])
    for cut in shards[1:]:
        factor_of = factor_of * one(*cut)
    return factor_of


def noise(stream_key, dims, deviation, limit, split=(), dtype=jnp.bfloat16):
    entries = jax.random.normal(stream_key, dims, jnp.float32) * deviation
    if len(split) > 0:
        entries = steps_of(stream_key, dims, split, -0.22, 0.18) * entries
    return jnp.clip(entries, min=-limit, max=limit).astype(dtype)


def noise_with(own_key, extent, spread, reach, cuts, heavy, held_as=jnp.bfloat16):
    drawn = spread * jax.random.normal(own_key, extent, jnp.float32)
    if cuts:
        drawn = drawn * steps_of(own_key, extent, cuts, -0.22, 0.18)
    return jnp.clip(strengthened(drawn, jax.random.fold_in(own_key, 3), *heavy), -reach, reach).astype(held_as)


def setup_inputs(seed: int = 0) -> dict:
    seeds = jax.random.split(jax.random.key(seed), 3)
    activations = noise(seeds[0], (SEQS, L, FF), 1.0, 6.0, ((0, 8), (2, 32)))
    out_grads = noise_with(seeds[1], (SEQS, L, D), 0.0625, 0.5, ((0, 8), (1, 32)), (0, 2, 8, 2.0))
    return dict(activations=activations, out_grads=out_grads)


def reference(activations, out_grads):
    def step(total, pair):
        acts, grads = pair
        grad = lax.dot_general(grads, acts, (((0,), (0,)), ((), ())), preferred_element_type=jnp.float32)
        return total + grad * grad, None

    start = jnp.zeros((out_grads.shape[2], activations.shape[2]), jnp.float32)
    total, _ = lax.scan(step, start, (activations, out_grads))
    return total / jnp.float32(SEQS)
```

```python
import functools

import jax
import jax.numpy as jnp
from jax import lax
from jax.experimental import pallas as pl
from jax.experimental.pallas import tpu as pltpu
from jax.sharding import Mesh, PartitionSpec as P

AXES = ("zlo", "x", "y", "zhi", "core")
SIZES = (2, 4, 4, 4, 2)
SEQS_DP = 3
ROWS = 16


def shift(value, axis, by):
    n = lax.axis_size(axis)
    return lax.ppermute(value, axis, [(i, (i + by) % n) for i in range(n)])


def square_sum(first, last, seqs, *refs):
    place, acts, grads, rest = refs[0], refs[1:5], refs[5:13], refs[13:]
    before, out, total = (None, *rest) if first else rest
    step = pl.program_id(0)
    half = grads[0].shape[-1]
    for source in range(4):
        rows = [
            acts[source][0, pl.ds(pl.multiple_of(place[k], ROWS), ROWS), :]
            for k in range(16)
        ]
        act = jnp.concatenate(rows, axis=0)
        for side in range(2):
            grad = jnp.concatenate(
                [grads[4 * side + k // 4][k % 4, source, 0] for k in range(16)], axis=0
            )
            part = lax.dot_general(
                grad, act, (((0,), (0,)), ((), ())), preferred_element_type=jnp.float32
            )
            at = slice(side * half, (side + 1) * half)
            if source == 0:

                @pl.when(step == 0)
                def _():
                    total[at, :] = part * part if first else before[at, :] + part * part

                @pl.when(step > 0)
                def _():
                    total[at, :] += part * part
            else:
                total[at, :] += part * part

    @pl.when(step == SEQS_DP - 1)
    def _():
        if not last:
            out[...] = total[...]
        else:
            core = place[16]
            for side, where in enumerate((core, 1 - core)):
                at = slice(side * half, (side + 1) * half)
                out[pl.ds(pl.multiple_of(where * half, half), half), :] = (
                    total[at, :] / jnp.float32(seqs)
                )


def add_group(last, seqs, place, acts, grads, before=None):
    _, tokens, feats = acts[0].shape
    half = grads[0].shape[-1]
    shape = (2 * half, feats)
    one = pl.Buffered(1)
    specs = [pl.BlockSpec(memory_space=pltpu.SMEM)]
    specs += [pl.BlockSpec((1, tokens, feats), lambda j: (j, 0, 0))] * 4
    specs += [pl.BlockSpec((4, 4, 1, ROWS, half), lambda j: (0, 0, j, 0, 0))] * 8
    args = [place, *acts, *grads]
    if before is not None:
        specs.append(pl.BlockSpec(shape, lambda j: (0, 0), pipeline_mode=one))
        args.append(before)
    return pl.pallas_call(
        functools.partial(square_sum, before is None, last, seqs),
        grid=(SEQS_DP,),
        in_specs=specs,
        out_specs=pl.BlockSpec(shape, lambda j: (0, 0), pipeline_mode=one),
        out_shape=jax.ShapeDtypeStruct(shape, jnp.float32),
        scratch_shapes=[pltpu.VMEM(shape, jnp.float32)],
        compiler_params=pltpu.CompilerParams(vmem_limit_bytes=56 * 2**20),
        cost_estimate=pl.CostEstimate(
            flops=2 * 12 * tokens * 2 * half * feats,
            bytes_accessed=16 * 2**20,
            transcendentals=0,
        ),
    )(*args)


def to_owner(block, core):
    block = block.transpose(3, 2, 0, 1, 4)
    mine = lax.dynamic_index_in_dim(block, core, 0, keepdims=False)
    other = lax.dynamic_index_in_dim(block, 1 - core, 0, keepdims=False)
    other = shift(other, "core", 1)
    low = jnp.where(core == 0, mine, other)
    high = jnp.where(core == 0, other, mine)
    both = jnp.concatenate([low, high], axis=2)
    x = lax.axis_index("x")

    def piece(by):
        return lax.dynamic_index_in_dim(both, (x + by) % 4, 0, keepdims=False)

    return jnp.stack(
        [piece(0), shift(piece(1), "x", 1), shift(piece(-1), "x", -1), shift(piece(2), "x", 2)]
    )


def ring(block, axis, on):
    below = shift(block, axis, 1)
    above = shift(block, axis, -1)
    far = shift(below, axis, 1) if on > 0 else shift(above, axis, -1)
    return [block, below, above, far]


def per_device(activations, out_grads):
    zlo, y, zhi, core = (lax.axis_index(a) for a in ("zlo", "y", "zhi", "core"))
    seq_dev, tokens, _ = activations.shape
    width = out_grads.shape[2]
    half = width // 16
    seqs = seq_dev * 8

    by_z = out_grads.reshape(seq_dev, out_grads.shape[1], 2, 4, 2, half)
    near = lax.dynamic_index_in_dim(by_z, zlo, 2, keepdims=False)
    away = lax.dynamic_index_in_dim(by_z, 1 - zlo, 2, keepdims=False)

    offsets = (0, -1, 1, 2)
    place = [
        ROWS * (((y + dy) % 4) * 4 + (zhi + dz) % 4) for dy in offsets for dz in offsets
    ]
    place = jnp.stack([*place, core]).astype(jnp.int32)

    total = None
    for group in range(2):
        on = 1 if group == 0 else -1
        acts = activations if group == 0 else shift(activations, "zlo", 1)
        block = near if group == 0 else shift(away, "zlo", 1)
        block = to_owner(block, core)
        column = jnp.stack(ring(block, "zhi", on))
        mine = ring(column, "y", on)
        theirs = [shift(part, "core", 1) for part in mine]
        total = add_group(
            group == 1, seqs, place, ring(acts, "x", on), [*mine, *theirs], total
        )
    return total


def solution(mesh):
    fine = Mesh(mesh.devices.reshape(SIZES), AXES)
    dp, tensor = AXES[:2], AXES[2:]
    placed = (P(dp, None, tensor), P(dp, tensor, None))
    return jax.shard_map(
        per_device, mesh=fine, in_specs=placed, out_specs=P(dp, tensor), check_vma=False
    )
```

```python
import functools

import jax
import jax.numpy as jnp
from jax import lax
from jax.experimental import pallas as pl
from jax.experimental.pallas import tpu as pltpu
from jax.sharding import Mesh, PartitionSpec as P

AXES = ("zlo", "x", "y", "zhi", "core")
SIZES = (2, 4, 4, 4, 2)
SEQS_DP = 3
ROWS = 16
LANES = 256
SCALE = 14
SWAP = (0, 2, 1, 3)
VMEM = pl.BlockSpec(memory_space=pltpu.VMEM)


def swap(value, axis):
    return lax.ppermute(value, axis, [(0, 1), (1, 0)])


def send(value, axis, by):
    pairs = [
        (2 * i + c, 2 * ((i + (by if c == 0 else -by)) % 4) + c)
        for i in range(4)
        for c in range(2)
    ]
    return lax.ppermute(value, (axis, "core"), pairs)


def level(values):
    return lax.optimization_barrier(values)


def order(blocks, other):
    at = SWAP if other else range(4)
    return [blocks[dy][dz] for dy in at for dz in at]


def turn_body(place, acts, out):
    rows = [acts[0, pl.ds(pl.multiple_of(place[k], ROWS), ROWS), :] for k in range(16)]
    out[0] = jnp.concatenate(rows, axis=0).T


def turn(place, acts):
    seqs, tokens, feats = acts.shape
    return pl.pallas_call(
        turn_body,
        grid=(seqs,),
        in_specs=[
            pl.BlockSpec(memory_space=pltpu.SMEM),
            pl.BlockSpec((1, tokens, feats), lambda j: (j, 0, 0)),
        ],
        out_specs=pl.BlockSpec((1, feats, tokens), lambda j: (j, 0, 0)),
        out_shape=jax.ShapeDtypeStruct((seqs, feats, tokens), acts.dtype),
        compiler_params=pltpu.CompilerParams(vmem_limit_bytes=6 * 2**20),
        cost_estimate=pl.CostEstimate(
            flops=10**9, bytes_accessed=4 * acts.size, transcendentals=0
        ),
    )(place, acts)


def square_sum(seqs, table, swapped, last, core, *refs):
    acts, refs = refs[:4], refs[4:]
    if last:
        grads, (before, *_, out, total, turned, sem) = refs[:3], refs[3:]
    else:
        grads, sent, total = refs[:-2], *refs[-2:]
    half = total.shape[1]
    if last:
        back = jnp.exp2(before[-8:, :][:1] - SCALE)

    def add(source, seq, first=False):
        act = acts[source][seq]
        there = SWAP[source] if swapped else source
        rows = [grads[at][(*index, there, seq)] for at, index in table]
        grad = jnp.concatenate(rows, axis=0)
        for n in range(half // LANES):
            part = jnp.dot(
                act,
                grad[:, n * LANES : (n + 1) * LANES],
                preferred_element_type=jnp.float32,
            )
            at = (slice(None), slice(n * LANES, (n + 1) * LANES))
            if not first:
                total[at] += part * part
            elif last:
                total[at] = before[: total.shape[0], at[1]] * back[:, at[1]] + part * part
            else:
                total[at] = part * part

    add(0, 0, first=True)
    for source in range(1, 4):
        add(source, 0)

    @pl.loop(1, SEQS_DP)
    def _(seq):
        for source in range(4):
            add(source, seq)

    if last:
        where = 1 - core[0] if swapped else core[0]
        turned[...] = total[...].T * jnp.float32(1 / seqs)
        at = pl.ds(pl.multiple_of(where * half, half), half)
        copy = pltpu.make_async_copy(turned, out.at[at, :], sem)
        copy.start()
        copy.wait()
    else:
        peak = jnp.max(total[...], axis=(0, 1), keepdims=True)
        exponent = jnp.floor(jnp.log2(jnp.maximum(peak, jnp.float32(1e-30))))
        sent[: total.shape[0], :] = total[...] * jnp.exp2(SCALE - exponent)
        sent[total.shape[0] :, :] = jnp.broadcast_to(exponent, (ROWS, half))


def add_side(seqs, core, acts, grads, table, swapped, before=None, out=None):
    _, feats, tokens = acts[0].shape
    half = grads[0].shape[-1]
    last = before is not None
    total = jax.ShapeDtypeStruct((feats, half), jnp.float32)
    args = [core, *acts, *grads]
    specs = [pl.BlockSpec(memory_space=pltpu.SMEM)] + [VMEM] * (len(args) - 1)
    anywhere = pl.BlockSpec(memory_space=pl.ANY)
    if last:
        args.append(before)
        specs.append(VMEM)
        if swapped:
            args.append(out)
            specs.append(anywhere)
        result = dict(
            out_shape=jax.ShapeDtypeStruct((2 * half, feats), jnp.float32),
            out_specs=anywhere,
            scratch_shapes=[
                pltpu.VMEM(total.shape, jnp.float32),
                pltpu.VMEM((half, feats), jnp.float32),
                pltpu.SemaphoreType.DMA,
            ],
            input_output_aliases={len(args) - 1: 0} if swapped else {},
        )
    else:
        result = dict(
            out_shape=jax.ShapeDtypeStruct((feats + ROWS, half), jnp.float32),
            out_specs=VMEM,
            scratch_shapes=[pltpu.VMEM(total.shape, jnp.float32)],
        )
    return pl.pallas_call(
        functools.partial(square_sum, seqs, table, swapped, last),
        in_specs=specs,
        compiler_params=pltpu.CompilerParams(vmem_limit_bytes=6 * 2**20),
        cost_estimate=pl.CostEstimate(
            flops=2 * 12 * tokens * half * feats,
            bytes_accessed=8 * 2**20,
            transcendentals=0,
        ),
        **result,
    )(*args)


def to_owner(grads, core, zlo, sources):
    seq_dev, rows, width = grads.shape
    block = grads.reshape(seq_dev, rows, 2, 4, 2, width // 16).transpose(4, 3, 2, 0, 1, 5)
    mine = lax.dynamic_index_in_dim(block, core, 0, keepdims=False)
    other = lax.dynamic_index_in_dim(block, 1 - core, 0, keepdims=False)
    other = swap(other, "core")
    low = jnp.where(core == 0, mine, other)
    high = jnp.where(core == 0, other, mine)
    both = jnp.concatenate([low, high], axis=3)
    both = lax.all_to_all(both, "x", 0, 0, tiled=True)

    def part(s, z):
        start = (s, z, 0, 0, 0)
        return lax.dynamic_slice(both, start, (1, 1, *both.shape[2:])).reshape(both.shape[2:])

    return jnp.stack([jnp.stack([part(s, z) for s in sources]) for z in (1 - zlo, zlo)])


def cross_zlo(total):
    return swap(total.astype(jnp.float16), "zlo")


def per_device(activations, out_grads):
    zlo, y, zhi, core = (lax.axis_index(a) for a in ("zlo", "y", "zhi", "core"))
    seq_dev, rows, width = out_grads.shape
    seqs = seq_dev * 8
    way = 1 - 2 * core
    offsets = (0, -way, way, 2)
    place = [
        ROWS * (((y + dy) % 4) * 4 + (zhi + dz) % 4) for dy in offsets for dz in offsets
    ]
    place = jnp.stack(place).astype(jnp.int32)
    which = jnp.reshape(core, (1,)).astype(jnp.int32)

    x = lax.axis_index("x")
    g = to_owner(out_grads, core, zlo, [(x + by) % 4 for by in offsets])
    acts = turn(place, activations)
    g, acts = level((g, acts))

    z1p, z1q = send(g[0], "zhi", 1), send(g[0], "zhi", -1)
    own_p, own_q = send(g, "y", 1), send(g, "y", -1)
    ap = send(acts, "x", 1)
    z1p, z1q, own_p, own_q, ap, g, acts = level((z1p, z1q, own_p, own_q, ap, g, acts))

    z1f = send(z1p, "zhi", 1)
    own_f = send(own_p, "y", 1)
    aq = send(acts, "x", -1)
    z1p, z1q, z1f, own_p, own_q, own_f, g = level(
        (z1p, z1q, z1f, own_p, own_q, own_f, g)
    )

    r1 = jnp.stack([z1p, z1q, z1f])
    y1p, y1q = send(r1, "y", 1), send(r1, "y", -1)
    z2p, z2q = send(g[1], "zhi", 1), send(g[1], "zhi", -1)
    r1, y1p, y1q, z2p, z2q, ap, aq, acts, own_p, own_q = level(
        (r1, y1p, y1q, z2p, z2q, ap, aq, acts, own_p, own_q)
    )

    z2f = send(z2p, "zhi", 1)
    w1p = jnp.concatenate([own_p[:1], y1p])
    y1f = send(y1p, "y", 1)
    af = send(ap, "x", 1)
    some1 = jnp.stack(
        [jnp.concatenate([g[:1], r1]), w1p, jnp.concatenate([own_q[:1], y1q])]
    )
    some1_t = swap(some1, "core")
    z2p, z2q, z2f, own_p, own_q, own_f, some1_t, y1f, af = level(
        (z2p, z2q, z2f, own_p, own_q, own_f, some1_t, y1f, af)
    )
    w1f = jnp.concatenate([own_f[:1], y1f])

    r2 = jnp.stack([z2p, z2q, z2f])
    y2p, y2q = send(r2, "y", 1), send(r2, "y", -1)
    some2 = jnp.stack([w1f, jnp.concatenate([g[1:], r2])])
    some2_t = swap(some2, "core")

    def whole(at, *index):
        return [(at, (*index, dz)) for dz in range(4)]

    acts = [acts, ap, aq, af]
    table = order([whole(0, 0), whole(0, 1), whole(0, 2), whole(1)], False)
    first = add_side(seqs, which, acts, [some1, w1f], table, False)
    first = cross_zlo(first)
    table = order([whole(0, 0), whole(0, 1), whole(0, 2), whole(1, 0)], True)
    second = add_side(seqs, which, acts, [some1_t, some2_t], table, True)
    first, second, y2p, y2q, own_p, own_q = level(
        (first, second, y2p, y2q, own_p, own_q)
    )

    y2f = send(y2p, "y", 1)
    second = cross_zlo(second)
    some3 = jnp.concatenate([own_p[1:], y2p, own_q[1:], y2q, own_f[1:]])
    some3_t = swap(some3, "core")
    second, y2f_tied = level((second, y2f))
    y2f_t = swap(y2f_tied, "core")

    def last_blocks():
        below = [(1, (dz,)) for dz in range(4)]
        above = [(1, (4 + dz,)) for dz in range(4)]
        return [whole(0, 1), below, above, [(1, (8,))] + [(2, (dz,)) for dz in range(3)]]

    table = order(last_blocks(), False)
    grads = [some2, some3, y2f]
    out = add_side(seqs, which, acts, grads, table, False, first.astype(jnp.float32))
    table = order(last_blocks(), True)
    grads = [some2_t, some3_t, y2f_t]
    return add_side(seqs, which, acts, grads, table, True, second.astype(jnp.float32), out)


def solution(mesh):
    fine = Mesh(mesh.devices.reshape(SIZES), AXES)
    dp, tensor = AXES[:2], AXES[2:]
    placed = (P(dp, None, tensor), P(dp, tensor, None))
    return jax.shard_map(
        per_device, mesh=fine, in_specs=placed, out_specs=P(dp, tensor), check_vma=False
    )
```

```python
import functools

import jax
import jax.numpy as jnp
from jax import lax
from jax.experimental import pallas as pl
from jax.experimental.pallas import tpu as pltpu
from jax.sharding import Mesh, PartitionSpec as P

AXES = ("zlo", "x", "y", "zhi", "core")
SIZES = (2, 4, 4, 4, 2)
SEQS_DP = 3
ROWS = 16
LANES = 256
SCALE = 14
SWAP = (0, 2, 1, 3)
VMEM = pl.BlockSpec(memory_space=pltpu.VMEM)


def swap(value, axis):
    return lax.ppermute(value, axis, [(0, 1), (1, 0)])


def send(value, axis, by):
    pairs = [
        (2 * i + c, 2 * ((i + (by if c == 0 else -by)) % 4) + c)
        for i in range(4)
        for c in range(2)
    ]
    return lax.ppermute(value, (axis, "core"), pairs)


def level(values):
    return lax.optimization_barrier(values)


def order(blocks, other):
    at = SWAP if other else range(4)
    return [blocks[dy][dz] for dy in at for dz in at]


def turn_body(place, acts, out):
    rows = [acts[0, pl.ds(pl.multiple_of(place[k], ROWS), ROWS), :] for k in range(16)]
    out[0] = jnp.concatenate(rows, axis=0).T


def turn(place, acts):
    seqs, tokens, feats = acts.shape
    return pl.pallas_call(
        turn_body,
        grid=(seqs,),
        in_specs=[
            pl.BlockSpec(memory_space=pltpu.SMEM),
            pl.BlockSpec((1, tokens, feats), lambda j: (j, 0, 0)),
        ],
        out_specs=pl.BlockSpec((1, feats, tokens), lambda j: (j, 0, 0)),
        out_shape=jax.ShapeDtypeStruct((seqs, feats, tokens), acts.dtype),
        compiler_params=pltpu.CompilerParams(vmem_limit_bytes=6 * 2**20),
        cost_estimate=pl.CostEstimate(
            flops=10**9, bytes_accessed=4 * acts.size, transcendentals=0
        ),
    )(place, acts)


def square_sum(seqs, table, swapped, last, sources, more, core, *refs):
    acts, refs = refs[: len(sources)], refs[len(sources) :]
    if last:
        grads, (before, *_, out, total, turned, sem) = refs[:3], refs[3:]
    else:
        grads, sent, total = refs[:2], *refs[-2:]
    half = total.shape[1]
    if last:
        back = jnp.exp2(before[-8:, :][:1] - SCALE)

    def add(source, seq, first=False):
        act = acts[sources.index(source)][seq]
        there = SWAP[source] if swapped else source
        rows = [grads[at][(*index, there, seq)] for at, index in table]
        grad = jnp.concatenate(rows, axis=0)
        for n in range(half // LANES):
            part = jnp.dot(
                act,
                grad[:, n * LANES : (n + 1) * LANES],
                preferred_element_type=jnp.float32,
            )
            at = (slice(None), slice(n * LANES, (n + 1) * LANES))
            if not first:
                total[at] += part * part
            elif last:
                total[at] = before[: total.shape[0], at[1]] * back[:, at[1]] + part * part
            elif more == "after":
                total[at] = refs[2][at] + part * part
            else:
                total[at] = part * part

    for source in sources:
        add(source, 0, first=source == sources[0])

    @pl.loop(1, SEQS_DP)
    def _(seq):
        for source in sources:
            add(source, seq)

    if last:
        where = 1 - core[0] if swapped else core[0]
        turned[...] = total[...].T * jnp.float32(1 / seqs)
        at = pl.ds(pl.multiple_of(where * half, half), half)
        copy = pltpu.make_async_copy(turned, out.at[at, :], sem)
        copy.start()
        copy.wait()
    elif more == "before":
        sent[...] = total[...]
    else:
        peak = jnp.max(total[...], axis=(0, 1), keepdims=True)
        exponent = jnp.floor(jnp.log2(jnp.maximum(peak, jnp.float32(1e-30))))
        sent[: total.shape[0], :] = total[...] * jnp.exp2(SCALE - exponent)
        sent[total.shape[0] :, :] = jnp.broadcast_to(exponent, (ROWS, half))


def add_side(
    seqs, core, acts, grads, table, swapped, before=None, out=None, sources=(0, 1, 2, 3), more=""
):
    acts = [acts[k] for k in sources]
    _, feats, tokens = acts[0].shape
    half = grads[0].shape[-1]
    last = before is not None and more != "after"
    total = jax.ShapeDtypeStruct((feats, half), jnp.float32)
    args = [core, *acts, *grads]
    specs = [pl.BlockSpec(memory_space=pltpu.SMEM)] + [VMEM] * (len(args) - 1)
    anywhere = pl.BlockSpec(memory_space=pl.ANY)
    if last:
        args.append(before)
        specs.append(VMEM)
        if swapped:
            args.append(out)
            specs.append(anywhere)
        result = dict(
            out_shape=jax.ShapeDtypeStruct((2 * half, feats), jnp.float32),
            out_specs=anywhere,
            scratch_shapes=[
                pltpu.VMEM(total.shape, jnp.float32),
                pltpu.VMEM((half, feats), jnp.float32),
                pltpu.SemaphoreType.DMA,
            ],
            input_output_aliases={len(args) - 1: 0} if swapped else {},
        )
    else:
        if more == "after":
            args.append(before)
            specs.append(VMEM)
        rows = feats + (0 if more == "before" else ROWS)
        result = dict(
            out_shape=jax.ShapeDtypeStruct((rows, half), jnp.float32),
            out_specs=VMEM,
            scratch_shapes=[pltpu.VMEM(total.shape, jnp.float32)],
        )
    return pl.pallas_call(
        functools.partial(square_sum, seqs, table, swapped, last, sources, more),
        in_specs=specs,
        compiler_params=pltpu.CompilerParams(vmem_limit_bytes=6 * 2**20),
        cost_estimate=pl.CostEstimate(
            flops=2 * 3 * len(sources) * tokens * half * feats,
            bytes_accessed=8 * 2**20,
            transcendentals=0,
        ),
        **result,
    )(*args)


def to_owner(grads, core, zlo):
    seq_dev, rows, width = grads.shape
    block = grads.reshape(seq_dev, rows, 2, 4, 2, width // 16).transpose(4, 3, 2, 0, 1, 5)
    mine = lax.dynamic_index_in_dim(block, core, 0, keepdims=False)
    other = lax.dynamic_index_in_dim(block, 1 - core, 0, keepdims=False)
    other = swap(other, "core")
    low = jnp.where(core == 0, mine, other)
    high = jnp.where(core == 0, other, mine)
    both = jnp.concatenate([low, high], axis=3)
    x = lax.axis_index("x")
    way = 1 - 2 * core

    def piece(by):
        return lax.dynamic_index_in_dim(both, (x + by) % 4, 0, keepdims=False)

    parts = [piece(0), send(piece(way), "x", 1), send(piece(-way), "x", -1)]
    parts = jnp.stack([*parts, send(piece(2), "x", 2)])
    return jnp.stack([lax.dynamic_index_in_dim(parts, z, 1, keepdims=False) for z in (1 - zlo, zlo)])


def cross_zlo(total):
    return swap(total.astype(jnp.float16), "zlo")


def per_device(activations, out_grads):
    zlo, y, zhi, core = (lax.axis_index(a) for a in ("zlo", "y", "zhi", "core"))
    seq_dev, rows, width = out_grads.shape
    seqs = seq_dev * 8
    way = 1 - 2 * core
    offsets = (0, -way, way, 2)
    place = [
        ROWS * (((y + dy) % 4) * 4 + (zhi + dz) % 4) for dy in offsets for dz in offsets
    ]
    place = jnp.stack(place).astype(jnp.int32)
    which = jnp.reshape(core, (1,)).astype(jnp.int32)

    g = to_owner(out_grads, core, zlo)
    acts = turn(place, activations)
    g, acts = level((g, acts))

    z1p, z1q = send(g[0], "zhi", 1), send(g[0], "zhi", -1)
    own_p, own_q = send(g, "y", 1), send(g, "y", -1)
    ap = send(acts, "x", 1)
    z1p, z1q, own_p, own_q, ap, g, acts = level((z1p, z1q, own_p, own_q, ap, g, acts))

    z1f = send(z1p, "zhi", 1)
    own_f = send(own_p, "y", 1)
    aq = send(acts, "x", -1)
    z1p, z1q, z1f, own_p, own_q, own_f, g = level(
        (z1p, z1q, z1f, own_p, own_q, own_f, g)
    )

    r1 = jnp.stack([z1p, z1q, z1f])
    y1p, y1q = send(r1, "y", 1), send(r1, "y", -1)
    z2p, z2q = send(g[1], "zhi", 1), send(g[1], "zhi", -1)
    r1, y1p, y1q, z2p, z2q, ap, aq, acts, own_p, own_q = level(
        (r1, y1p, y1q, z2p, z2q, ap, aq, acts, own_p, own_q)
    )

    z2f = send(z2p, "zhi", 1)
    w1p = jnp.concatenate([own_p[:1], y1p])
    y1f = send(y1p, "y", 1)
    af = send(ap, "x", 1)
    some1 = jnp.stack(
        [jnp.concatenate([g[:1], r1]), w1p, jnp.concatenate([own_q[:1], y1q])]
    )
    some1_t = swap(some1, "core")
    w1f = jnp.concatenate([own_f[:1], y1f])

    def whole(at, *index):
        return [(at, (*index, dz)) for dz in range(4)]

    acts = [acts, ap, aq, af]
    table = order([whole(0, 0), whole(0, 1), whole(0, 2), whole(1)], False)
    first = add_side(
        seqs, which, acts, [some1, w1f], table, False, None, None, (0, 1, 2), "before"
    )
    z2p, z2q, z2f, own_p, own_q, some1_t, first, acts = level(
        (z2p, z2q, z2f, own_p, own_q, some1_t, first, acts)
    )

    r2 = jnp.stack([z2p, z2q, z2f])
    y2p, y2q = send(r2, "y", 1), send(r2, "y", -1)
    some2 = jnp.stack([w1f, jnp.concatenate([g[1:], r2])])
    some2_t = swap(some2, "core")

    first = add_side(
        seqs, which, acts, [some1, w1f], table, False, first, None, (3,), "after"
    )
    first = cross_zlo(first)
    table = order([whole(0, 0), whole(0, 1), whole(0, 2), whole(1, 0)], True)
    second = add_side(seqs, which, acts, [some1_t, some2_t], table, True)
    first, second, y2p, y2q, own_p, own_q = level(
        (first, second, y2p, y2q, own_p, own_q)
    )

    y2f = send(y2p, "y", 1)
    second = cross_zlo(second)
    some3 = jnp.concatenate([own_p[1:], y2p, own_q[1:], y2q, own_f[1:]])
    some3_t = swap(some3, "core")
    def last_blocks():
        below = [(1, (dz,)) for dz in range(4)]
        above = [(1, (4 + dz,)) for dz in range(4)]
        return [whole(0, 1), below, above, [(1, (8,))] + [(2, (dz,)) for dz in range(3)]]

    table = order(last_blocks(), False)
    grads = [some2, some3, y2f]
    out = add_side(seqs, which, acts, grads, table, False, first.astype(jnp.float32))
    second, y2f, out = level((second, y2f, out))
    y2f_t = swap(y2f, "core")
    table = order(last_blocks(), True)
    grads = [some2_t, some3_t, y2f_t]
    return add_side(seqs, which, acts, grads, table, True, second.astype(jnp.float32), out)


def solution(mesh):
    fine = Mesh(mesh.devices.reshape(SIZES), AXES)
    dp, tensor = AXES[:2], AXES[2:]
    placed = (P(dp, None, tensor), P(dp, tensor, None))
    return jax.shard_map(
        per_device, mesh=fine, in_specs=placed, out_specs=P(dp, tensor), check_vma=False
    )
```

```python
import functools

import jax
import jax.numpy as jnp
from jax import lax
from jax.experimental import pallas as pl
from jax.experimental.pallas import tpu as pltpu
from jax.sharding import Mesh, PartitionSpec as P

AXES = ("zlo", "x", "y", "zhi", "core")
SIZES = (2, 4, 4, 4, 2)
SEQS_DP = 3
ROWS = 16
LANES = 256
SCALE = 14
SWAP = (0, 2, 1, 3)
VMEM = pl.BlockSpec(memory_space=pltpu.VMEM)


def swap(value, axis):
    return lax.ppermute(value, axis, [(0, 1), (1, 0)])


def send(value, axis, by):
    pairs = [
        (2 * i + c, 2 * ((i + (by if c == 0 else -by)) % 4) + c)
        for i in range(4)
        for c in range(2)
    ]
    return lax.ppermute(value, (axis, "core"), pairs)


def level(values):
    return lax.optimization_barrier(values)


def order(blocks, other):
    at = SWAP if other else range(4)
    return [blocks[dy][dz] for dy in at for dz in at]


def turn_body(place, acts, out):
    rows = [acts[0, pl.ds(pl.multiple_of(place[k], ROWS), ROWS), :] for k in range(16)]
    out[0] = jnp.concatenate(rows, axis=0).T


def turn(place, acts):
    seqs, tokens, feats = acts.shape
    return pl.pallas_call(
        turn_body,
        grid=(seqs,),
        in_specs=[
            pl.BlockSpec(memory_space=pltpu.SMEM),
            pl.BlockSpec((1, tokens, feats), lambda j: (j, 0, 0)),
        ],
        out_specs=pl.BlockSpec((1, feats, tokens), lambda j: (j, 0, 0)),
        out_shape=jax.ShapeDtypeStruct((seqs, feats, tokens), acts.dtype),
        compiler_params=pltpu.CompilerParams(vmem_limit_bytes=6 * 2**20),
        cost_estimate=pl.CostEstimate(
            flops=10**9, bytes_accessed=4 * acts.size, transcendentals=0
        ),
    )(place, acts)


def square_sum(seqs, table, swapped, last, sources, more, count, core, *refs):
    acts, refs = refs[: len(sources)], refs[len(sources) :]
    if last:
        grads, (before, *_, out, total, turned, sem) = refs[:3], refs[3:]
    else:
        grads, sent, total = refs[:count], *refs[-2:]
    half = total.shape[1]
    if last:
        back = jnp.exp2(before[-8:, :][:1] - SCALE)

    def add(source, seq, first=False):
        act = acts[sources.index(source)][seq]
        there = SWAP[source] if swapped else source
        rows = [grads[at][(*index, there, seq)] for at, index in table]
        grad = jnp.concatenate(rows, axis=0)
        for n in range(half // LANES):
            part = jnp.dot(
                act,
                grad[:, n * LANES : (n + 1) * LANES],
                preferred_element_type=jnp.float32,
            )
            at = (slice(None), slice(n * LANES, (n + 1) * LANES))
            if not first:
                total[at] += part * part
            elif last:
                total[at] = before[: total.shape[0], at[1]] * back[:, at[1]] + part * part
            elif more == "after":
                total[at] = refs[count][at] + part * part
            else:
                total[at] = part * part

    for source in sources:
        add(source, 0, first=source == sources[0])

    @pl.loop(1, SEQS_DP)
    def _(seq):
        for source in sources:
            add(source, seq)

    if last:
        where = 1 - core[0] if swapped else core[0]
        turned[...] = total[...].T * jnp.float32(1 / seqs)
        at = pl.ds(pl.multiple_of(where * half, half), half)
        copy = pltpu.make_async_copy(turned, out.at[at, :], sem)
        copy.start()
        copy.wait()
    elif more == "before":
        sent[...] = total[...]
    else:
        peak = jnp.max(total[...], axis=(0, 1), keepdims=True)
        exponent = jnp.floor(jnp.log2(jnp.maximum(peak, jnp.float32(1e-30))))
        sent[: total.shape[0], :] = total[...] * jnp.exp2(SCALE - exponent)
        sent[total.shape[0] :, :] = jnp.broadcast_to(exponent, (ROWS, half))


def add_side(
    seqs, core, acts, grads, table, swapped, before=None, out=None, sources=(0, 1, 2, 3), more=""
):
    acts = [acts[k] for k in sources]
    _, feats, tokens = acts[0].shape
    half = grads[0].shape[-1]
    last = before is not None and more != "after"
    total = jax.ShapeDtypeStruct((feats, half), jnp.float32)
    args = [core, *acts, *grads]
    specs = [pl.BlockSpec(memory_space=pltpu.SMEM)] + [VMEM] * (len(args) - 1)
    anywhere = pl.BlockSpec(memory_space=pl.ANY)
    if last:
        args.append(before)
        specs.append(VMEM)
        if swapped:
            args.append(out)
            specs.append(anywhere)
        result = dict(
            out_shape=jax.ShapeDtypeStruct((2 * half, feats), jnp.float32),
            out_specs=anywhere,
            scratch_shapes=[
                pltpu.VMEM(total.shape, jnp.float32),
                pltpu.VMEM((half, feats), jnp.float32),
                pltpu.SemaphoreType.DMA,
            ],
            input_output_aliases={len(args) - 1: 0} if swapped else {},
        )
    else:
        if more == "after":
            args.append(before)
            specs.append(VMEM)
        rows = feats + (0 if more == "before" else ROWS)
        result = dict(
            out_shape=jax.ShapeDtypeStruct((rows, half), jnp.float32),
            out_specs=VMEM,
            scratch_shapes=[pltpu.VMEM(total.shape, jnp.float32)],
        )
    return pl.pallas_call(
        functools.partial(square_sum, seqs, table, swapped, last, sources, more, len(grads)),
        in_specs=specs,
        compiler_params=pltpu.CompilerParams(vmem_limit_bytes=6 * 2**20),
        cost_estimate=pl.CostEstimate(
            flops=2 * 3 * len(sources) * tokens * half * feats,
            bytes_accessed=8 * 2**20,
            transcendentals=0,
        ),
        **result,
    )(*args)


def finish_body(seqs, core, total, before, token, given, out, turned, sem):
    half = total.shape[1]
    back = jnp.exp2(before[-8:, :][:1] - SCALE)
    whole = total[...] + before[: total.shape[0], :] * back
    turned[...] = whole.T * jnp.float32(1 / seqs)
    at = pl.ds(pl.multiple_of((1 - core[0]) * half, half), half)
    copy = pltpu.make_async_copy(turned, out.at[at, :], sem)
    copy.start()
    copy.wait()


def finish(seqs, core, total, before, token, out):
    feats, half = total.shape
    anywhere = pl.BlockSpec(memory_space=pl.ANY)
    return pl.pallas_call(
        functools.partial(finish_body, seqs),
        in_specs=[pl.BlockSpec(memory_space=pltpu.SMEM), VMEM, VMEM, anywhere, anywhere],
        out_specs=anywhere,
        out_shape=jax.ShapeDtypeStruct(out.shape, jnp.float32),
        scratch_shapes=[pltpu.VMEM((half, feats), jnp.float32), pltpu.SemaphoreType.DMA],
        input_output_aliases={4: 0},
        compiler_params=pltpu.CompilerParams(vmem_limit_bytes=6 * 2**20),
    )(core, total, before, token, out)


def to_owner(grads, core, zlo):
    seq_dev, rows, width = grads.shape
    block = grads.reshape(seq_dev, rows, 2, 4, 2, width // 16).transpose(4, 3, 2, 0, 1, 5)
    mine = lax.dynamic_index_in_dim(block, core, 0, keepdims=False)
    other = lax.dynamic_index_in_dim(block, 1 - core, 0, keepdims=False)
    other = swap(other, "core")
    low = jnp.where(core == 0, mine, other)
    high = jnp.where(core == 0, other, mine)
    both = jnp.concatenate([low, high], axis=3)
    x = lax.axis_index("x")
    way = 1 - 2 * core

    def piece(by):
        return lax.dynamic_index_in_dim(both, (x + by) % 4, 0, keepdims=False)

    parts = [piece(0), send(piece(way), "x", 1), send(piece(-way), "x", -1)]
    parts = jnp.stack([*parts, send(piece(2), "x", 2)])
    return jnp.stack([lax.dynamic_index_in_dim(parts, z, 1, keepdims=False) for z in (1 - zlo, zlo)])


def cross_zlo(total):
    return swap(total.astype(jnp.float16), "zlo")


def per_device(activations, out_grads):
    zlo, y, zhi, core = (lax.axis_index(a) for a in ("zlo", "y", "zhi", "core"))
    seq_dev, rows, width = out_grads.shape
    seqs = seq_dev * 8
    way = 1 - 2 * core
    offsets = (0, -way, way, 2)
    place = [
        ROWS * (((y + dy) % 4) * 4 + (zhi + dz) % 4) for dy in offsets for dz in offsets
    ]
    place = jnp.stack(place).astype(jnp.int32)
    which = jnp.reshape(core, (1,)).astype(jnp.int32)

    g = to_owner(out_grads, core, zlo)
    acts = turn(place, activations)
    g, acts = level((g, acts))

    z1p, z1q = send(g[0], "zhi", 1), send(g[0], "zhi", -1)
    own_p, own_q = send(g, "y", 1), send(g, "y", -1)
    ap = send(acts, "x", 1)
    z1p, z1q, own_p, own_q, ap, g, acts = level((z1p, z1q, own_p, own_q, ap, g, acts))

    z1f = send(z1p, "zhi", 1)
    own_f = send(own_p, "y", 1)
    aq = send(acts, "x", -1)
    z1p, z1q, z1f, own_p, own_q, own_f, g = level(
        (z1p, z1q, z1f, own_p, own_q, own_f, g)
    )

    r1 = jnp.stack([z1p, z1q, z1f])
    y1p, y1q = send(r1, "y", 1), send(r1, "y", -1)
    z2p, z2q = send(g[1], "zhi", 1), send(g[1], "zhi", -1)
    r1, y1p, y1q, z2p, z2q, ap, aq, acts, own_p, own_q = level(
        (r1, y1p, y1q, z2p, z2q, ap, aq, acts, own_p, own_q)
    )

    z2f = send(z2p, "zhi", 1)
    w1p = jnp.concatenate([own_p[:1], y1p])
    y1f = send(y1p, "y", 1)
    af = send(ap, "x", 1)
    some1 = jnp.stack(
        [jnp.concatenate([g[:1], r1]), w1p, jnp.concatenate([own_q[:1], y1q])]
    )
    some1_t = swap(some1, "core")
    w1f = jnp.concatenate([own_f[:1], y1f])

    def whole(at, *index):
        return [(at, (*index, dz)) for dz in range(4)]

    acts = [acts, ap, aq, af]
    table = order([whole(0, 0), whole(0, 1), whole(0, 2), whole(1)], False)
    first = add_side(
        seqs, which, acts, [some1, w1f], table, False, None, None, (0, 1, 2), "before"
    )
    z2p, z2q, z2f, own_p, own_q, some1_t, first, acts = level(
        (z2p, z2q, z2f, own_p, own_q, some1_t, first, acts)
    )

    r2 = jnp.stack([z2p, z2q, z2f])
    y2p, y2q = send(r2, "y", 1), send(r2, "y", -1)
    some2 = jnp.stack([w1f, jnp.concatenate([g[1:], r2])])
    some2_t = swap(some2, "core")

    first = add_side(
        seqs, which, acts, [some1, w1f], table, False, first, None, (3,), "after"
    )
    first = cross_zlo(first)
    table = order([whole(0, 0), whole(0, 1), whole(0, 2), whole(1, 0)], True)
    second = add_side(seqs, which, acts, [some1_t, some2_t], table, True)
    first, second, y2p, y2q, own_p, own_q = level(
        (first, second, y2p, y2q, own_p, own_q)
    )

    y2f = send(y2p, "y", 1)
    second = cross_zlo(second)
    some3 = jnp.concatenate([own_p[1:], y2p, own_q[1:], y2q, own_f[1:]])
    some3_t = swap(some3, "core")
    def last_blocks():
        below = [(1, (dz,)) for dz in range(4)]
        above = [(1, (4 + dz,)) for dz in range(4)]
        return [whole(0, 1), below, above, [(1, (8,))] + [(2, (dz,)) for dz in range(3)]]

    table = order(last_blocks(), False)
    grads = [some2, some3, y2f]
    out = add_side(seqs, which, acts, grads, table, False, first.astype(jnp.float32))
    y2f_t = swap(y2f, "core")
    second, out = level((second, out))
    token = swap(second[-ROWS:, :128].astype(jnp.float32), "core")
    table = order(last_blocks(), True)
    grads = [some2_t, some3_t, y2f_t]
    rest = add_side(seqs, which, acts, grads, table, True, more="before")
    second, token, rest = level((second, token, rest))
    return finish(seqs, which, rest, second.astype(jnp.float32), token, out)


def solution(mesh):
    fine = Mesh(mesh.devices.reshape(SIZES), AXES)
    dp, tensor = AXES[:2], AXES[2:]
    placed = (P(dp, None, tensor), P(dp, tensor, None))
    return jax.shard_map(
        per_device, mesh=fine, in_specs=placed, out_specs=P(dp, tensor), check_vma=False
    )
```

```python
import functools

import jax
import jax.numpy as jnp
from jax import lax
from jax.experimental import pallas as pl
from jax.experimental.pallas import tpu as pltpu
from jax.sharding import Mesh, PartitionSpec as P

AXES = ("zlo", "x", "y", "zhi", "core")
SIZES = (2, 4, 4, 4, 2)
SEQS_DP = 3
ROWS = 16
LANES = 256
PARTS = 4
SCALE = 14
SWAP = (0, 2, 1, 3)
VMEM = pl.BlockSpec(memory_space=pltpu.VMEM)


def swap(value, axis):
    return lax.ppermute(value, axis, [(0, 1), (1, 0)])


def send(value, axis, by):
    pairs = [
        (2 * i + c, 2 * ((i + (by if c == 0 else -by)) % 4) + c)
        for i in range(4)
        for c in range(2)
    ]
    return lax.ppermute(value, (axis, "core"), pairs)


def level(values):
    return lax.optimization_barrier(values)


def order(blocks, other):
    at = SWAP if other else range(4)
    return [blocks[dy][dz] for dy in at for dz in at]


def turn_body(place, acts, out):
    rows = [acts[0, pl.ds(pl.multiple_of(place[k], ROWS), ROWS), :] for k in range(16)]
    out[0] = jnp.concatenate(rows, axis=0).T


def turn(place, acts):
    seqs, tokens, feats = acts.shape
    return pl.pallas_call(
        turn_body,
        grid=(seqs,),
        in_specs=[
            pl.BlockSpec(memory_space=pltpu.SMEM),
            pl.BlockSpec((1, tokens, feats), lambda j: (j, 0, 0)),
        ],
        out_specs=pl.BlockSpec((1, feats, tokens), lambda j: (j, 0, 0)),
        out_shape=jax.ShapeDtypeStruct((seqs, feats, tokens), acts.dtype),
        compiler_params=pltpu.CompilerParams(vmem_limit_bytes=6 * 2**20),
        cost_estimate=pl.CostEstimate(
            flops=10**9, bytes_accessed=4 * acts.size, transcendentals=0
        ),
    )(place, acts)


def write_out(total, turned, out, sems, where, seqs):
    half = total.shape[1]
    size = half // PARTS
    copies = []
    for part in range(PARTS):
        rows = slice(part * size, (part + 1) * size)
        turned[rows, :] = total[:, rows].T * jnp.float32(1 / seqs)
        at = pl.ds(pl.multiple_of(where * half + part * size, size), size)
        copies.append(pltpu.make_async_copy(turned.at[rows, :], out.at[at, :], sems.at[part]))
        copies[-1].start()
    for copy in copies:
        copy.wait()


def square_sum(seqs, table, swapped, last, sources, more, count, core, *refs):
    acts, refs = refs[: len(sources)], refs[len(sources) :]
    if last:
        grads, (before, *_, out, total, turned, sem) = refs[:3], refs[3:]
    else:
        grads, sent, total = refs[:count], *refs[-2:]
    half = total.shape[1]
    if last:
        back = jnp.exp2(before[-8:, :][:1] - SCALE)

    def add(source, seq, first=False):
        act = acts[sources.index(source)][seq]
        there = SWAP[source] if swapped else source
        rows = [grads[at][(*index, there, seq)] for at, index in table]
        grad = jnp.concatenate(rows, axis=0)
        for n in range(half // LANES):
            part = jnp.dot(
                act,
                grad[:, n * LANES : (n + 1) * LANES],
                preferred_element_type=jnp.float32,
            )
            at = (slice(None), slice(n * LANES, (n + 1) * LANES))
            if not first:
                total[at] += part * part
            elif last:
                total[at] = before[: total.shape[0], at[1]] * back[:, at[1]] + part * part
            elif more == "after":
                total[at] = refs[count][at] + part * part
            else:
                total[at] = part * part

    for source in sources:
        add(source, 0, first=source == sources[0])

    @pl.loop(1, SEQS_DP)
    def _(seq):
        for source in sources:
            add(source, seq)

    if last:
        where = 1 - core[0] if swapped else core[0]
        write_out(total, turned, out, sem, where, seqs)
    elif more == "before":
        sent[...] = total[...]
    else:
        peak = jnp.max(total[...], axis=(0, 1), keepdims=True)
        exponent = jnp.floor(jnp.log2(jnp.maximum(peak, jnp.float32(1e-30))))
        sent[: total.shape[0], :] = total[...] * jnp.exp2(SCALE - exponent)
        sent[total.shape[0] :, :] = jnp.broadcast_to(exponent, (ROWS, half))


def add_side(
    seqs, core, acts, grads, table, swapped, before=None, out=None, sources=(0, 1, 2, 3), more=""
):
    acts = [acts[k] for k in sources]
    _, feats, tokens = acts[0].shape
    half = grads[0].shape[-1]
    last = before is not None and more != "after"
    total = jax.ShapeDtypeStruct((feats, half), jnp.float32)
    args = [core, *acts, *grads]
    specs = [pl.BlockSpec(memory_space=pltpu.SMEM)] + [VMEM] * (len(args) - 1)
    anywhere = pl.BlockSpec(memory_space=pl.ANY)
    if last:
        args.append(before)
        specs.append(VMEM)
        if swapped:
            args.append(out)
            specs.append(anywhere)
        result = dict(
            out_shape=jax.ShapeDtypeStruct((2 * half, feats), jnp.float32),
            out_specs=anywhere,
            scratch_shapes=[
                pltpu.VMEM(total.shape, jnp.float32),
                pltpu.VMEM((half, feats), jnp.float32),
                pltpu.SemaphoreType.DMA((PARTS,)),
            ],
            input_output_aliases={len(args) - 1: 0} if swapped else {},
        )
    else:
        if more == "after":
            args.append(before)
            specs.append(VMEM)
        rows = feats + (0 if more == "before" else ROWS)
        result = dict(
            out_shape=jax.ShapeDtypeStruct((rows, half), jnp.float32),
            out_specs=VMEM,
            scratch_shapes=[pltpu.VMEM(total.shape, jnp.float32)],
        )
    return pl.pallas_call(
        functools.partial(square_sum, seqs, table, swapped, last, sources, more, len(grads)),
        in_specs=specs,
        compiler_params=pltpu.CompilerParams(vmem_limit_bytes=6 * 2**20),
        cost_estimate=pl.CostEstimate(
            flops=2 * 3 * len(sources) * tokens * half * feats,
            bytes_accessed=8 * 2**20,
            transcendentals=0,
        ),
        **result,
    )(*args)


def finish_body(seqs, core, given_total, before, token, given, out, turned, sem, total):
    back = jnp.exp2(before[-8:, :][:1] - SCALE)
    total[...] = given_total[...] + before[: total.shape[0], :] * back
    write_out(total, turned, out, sem, 1 - core[0], seqs)


def finish(seqs, core, total, before, token, out):
    feats, half = total.shape
    anywhere = pl.BlockSpec(memory_space=pl.ANY)
    return pl.pallas_call(
        functools.partial(finish_body, seqs),
        in_specs=[pl.BlockSpec(memory_space=pltpu.SMEM), VMEM, VMEM, anywhere, anywhere],
        out_specs=anywhere,
        out_shape=jax.ShapeDtypeStruct(out.shape, jnp.float32),
        scratch_shapes=[
            pltpu.VMEM((half, feats), jnp.float32),
            pltpu.SemaphoreType.DMA((PARTS,)),
            pltpu.VMEM((feats, half), jnp.float32),
        ],
        input_output_aliases={4: 0},
        compiler_params=pltpu.CompilerParams(vmem_limit_bytes=6 * 2**20),
    )(core, total, before, token, out)


def to_owner(grads, core, zlo):
    seq_dev, rows, width = grads.shape
    block = grads.reshape(seq_dev, rows, 2, 4, 2, width // 16).transpose(4, 3, 2, 0, 1, 5)
    mine = lax.dynamic_index_in_dim(block, core, 0, keepdims=False)
    other = lax.dynamic_index_in_dim(block, 1 - core, 0, keepdims=False)
    other = swap(other, "core")
    low = jnp.where(core == 0, mine, other)
    high = jnp.where(core == 0, other, mine)
    both = jnp.concatenate([low, high], axis=3)
    x = lax.axis_index("x")
    way = 1 - 2 * core

    def piece(by):
        return lax.dynamic_index_in_dim(both, (x + by) % 4, 0, keepdims=False)

    parts = [piece(0), send(piece(way), "x", 1), send(piece(-way), "x", -1)]
    parts = jnp.stack([*parts, send(piece(2), "x", 2)])
    return jnp.stack([lax.dynamic_index_in_dim(parts, z, 1, keepdims=False) for z in (1 - zlo, zlo)])


def cross_zlo(total):
    return swap(total.astype(jnp.float16), "zlo")


def per_device(activations, out_grads):
    zlo, y, zhi, core = (lax.axis_index(a) for a in ("zlo", "y", "zhi", "core"))
    seq_dev, rows, width = out_grads.shape
    seqs = seq_dev * 8
    way = 1 - 2 * core
    offsets = (0, -way, way, 2)
    place = [
        ROWS * (((y + dy) % 4) * 4 + (zhi + dz) % 4) for dy in offsets for dz in offsets
    ]
    place = jnp.stack(place).astype(jnp.int32)
    which = jnp.reshape(core, (1,)).astype(jnp.int32)

    g = to_owner(out_grads, core, zlo)
    acts = turn(place, activations)
    g, acts = level((g, acts))

    z1p, z1q = send(g[0], "zhi", 1), send(g[0], "zhi", -1)
    own_p, own_q = send(g, "y", 1), send(g, "y", -1)
    ap = send(acts, "x", 1)
    z1p, z1q, own_p, own_q, ap, g, acts = level((z1p, z1q, own_p, own_q, ap, g, acts))

    z1f = send(z1p, "zhi", 1)
    own_f = send(own_p, "y", 1)
    aq = send(acts, "x", -1)
    z1p, z1q, z1f, own_p, own_q, own_f, g = level(
        (z1p, z1q, z1f, own_p, own_q, own_f, g)
    )

    r1 = jnp.stack([z1p, z1q, z1f])
    y1p, y1q = send(r1, "y", 1), send(r1, "y", -1)
    z2p, z2q = send(g[1], "zhi", 1), send(g[1], "zhi", -1)
    r1, y1p, y1q, z2p, z2q, ap, aq, acts, own_p, own_q = level(
        (r1, y1p, y1q, z2p, z2q, ap, aq, acts, own_p, own_q)
    )

    z2f = send(z2p, "zhi", 1)
    w1p = jnp.concatenate([own_p[:1], y1p])
    y1f = send(y1p, "y", 1)
    af = send(ap, "x", 1)
    some1 = jnp.stack(
        [jnp.concatenate([g[:1], r1]), w1p, jnp.concatenate([own_q[:1], y1q])]
    )
    some1_t = swap(some1, "core")
    w1f = jnp.concatenate([own_f[:1], y1f])

    def whole(at, *index):
        return [(at, (*index, dz)) for dz in range(4)]

    acts = [acts, ap, aq, af]
    table = order([whole(0, 0), whole(0, 1), whole(0, 2), whole(1)], False)
    first = add_side(
        seqs, which, acts, [some1, w1f], table, False, None, None, (0, 1, 2), "before"
    )
    z2p, z2q, z2f, own_p, own_q, some1_t, first, acts = level(
        (z2p, z2q, z2f, own_p, own_q, some1_t, first, acts)
    )

    r2 = jnp.stack([z2p, z2q, z2f])
    y2p, y2q = send(r2, "y", 1), send(r2, "y", -1)
    some2 = jnp.stack([w1f, jnp.concatenate([g[1:], r2])])
    some2_t = swap(some2, "core")

    first = add_side(
        seqs, which, acts, [some1, w1f], table, False, first, None, (3,), "after"
    )
    first = cross_zlo(first)
    table = order([whole(0, 0), whole(0, 1), whole(0, 2), whole(1, 0)], True)
    second = add_side(seqs, which, acts, [some1_t, some2_t], table, True)
    first, second, y2p, y2q, own_p, own_q = level(
        (first, second, y2p, y2q, own_p, own_q)
    )

    y2f = send(y2p, "y", 1)
    second = cross_zlo(second)
    some3 = jnp.concatenate([own_p[1:], y2p, own_q[1:], y2q, own_f[1:]])
    some3_t = swap(some3, "core")
    def last_blocks():
        below = [(1, (dz,)) for dz in range(4)]
        above = [(1, (4 + dz,)) for dz in range(4)]
        return [whole(0, 1), below, above, [(1, (8,))] + [(2, (dz,)) for dz in range(3)]]

    table = order(last_blocks(), False)
    grads = [some2, some3, y2f]
    out = add_side(seqs, which, acts, grads, table, False, first.astype(jnp.float32))
    y2f_t = swap(y2f, "core")
    second, out = level((second, out))
    token = swap(second[-ROWS:, :128].astype(jnp.float32), "core")
    table = order(last_blocks(), True)
    grads = [some2_t, some3_t, y2f_t]
    rest = add_side(seqs, which, acts, grads, table, True, more="before")
    second, token, rest = level((second, token, rest))
    return finish(seqs, which, rest, second.astype(jnp.float32), token, out)


def solution(mesh):
    fine = Mesh(mesh.devices.reshape(SIZES), AXES)
    dp, tensor = AXES[:2], AXES[2:]
    placed = (P(dp, None, tensor), P(dp, tensor, None))
    return jax.shard_map(
        per_device, mesh=fine, in_specs=placed, out_specs=P(dp, tensor), check_vma=False
    )
```

```python
import functools

import jax
import jax.numpy as jnp
from jax import lax
from jax.experimental import pallas as pl
from jax.experimental.pallas import tpu as pltpu
from jax.sharding import Mesh, PartitionSpec as P

AXES = ("zlo", "x", "y", "zhi", "core")
SIZES = (2, 4, 4, 4, 2)
SEQS_DP = 3
ROWS = 16
LANES = 256
PARTS = 4
SCALE = 14
SWAP = (0, 2, 1, 3)
VMEM = pl.BlockSpec(memory_space=pltpu.VMEM)


def swap(value, axis):
    return lax.ppermute(value, axis, [(0, 1), (1, 0)])


def send(value, axis, by):
    pairs = [
        (2 * i + c, 2 * ((i + (by if c == 0 else -by)) % 4) + c)
        for i in range(4)
        for c in range(2)
    ]
    return lax.ppermute(value, (axis, "core"), pairs)


def level(values):
    return lax.optimization_barrier(values)


def order(blocks, other):
    at = SWAP if other else range(4)
    return [blocks[dy][dz] for dy in at for dz in at]


def turn_body(place, acts, out):
    rows = [acts[0, pl.ds(pl.multiple_of(place[k], ROWS), ROWS), :] for k in range(16)]
    out[0] = jnp.concatenate(rows, axis=0).T


def turn(place, acts):
    seqs, tokens, feats = acts.shape
    return pl.pallas_call(
        turn_body,
        grid=(seqs,),
        in_specs=[
            pl.BlockSpec(memory_space=pltpu.SMEM),
            pl.BlockSpec((1, tokens, feats), lambda j: (j, 0, 0)),
        ],
        out_specs=pl.BlockSpec((1, feats, tokens), lambda j: (j, 0, 0)),
        out_shape=jax.ShapeDtypeStruct((seqs, feats, tokens), acts.dtype),
        compiler_params=pltpu.CompilerParams(vmem_limit_bytes=6 * 2**20),
        cost_estimate=pl.CostEstimate(
            flops=10**9, bytes_accessed=4 * acts.size, transcendentals=0
        ),
    )(place, acts)


def write_out(total, turned, out, sems, where, seqs):
    half = total.shape[1]
    size = half // PARTS
    copies = []
    for part in range(PARTS):
        rows = slice(part * size, (part + 1) * size)
        turned[rows, :] = total[:, rows].T * jnp.float32(1 / seqs)
        at = pl.ds(pl.multiple_of(where * half + part * size, size), size)
        copies.append(pltpu.make_async_copy(turned.at[rows, :], out.at[at, :], sems.at[part]))
        copies[-1].start()
    for copy in copies:
        copy.wait()


def square_sum(seqs, table, swapped, last, sources, more, count, core, *refs):
    acts, refs = refs[: len(sources)], refs[len(sources) :]
    if last:
        grads, (before, *_, out, total, turned, sem) = refs[:3], refs[3:]
    else:
        grads, sent, total = refs[:count], *refs[-2:]
        total = sent if more == "before" else total
    half = total.shape[1]
    if last:
        back = jnp.exp2(before[-8:, :][:1] - SCALE)

    def add(source, seq, first=False):
        act = acts[sources.index(source)][seq]
        there = SWAP[source] if swapped else source
        rows = [grads[at][(*index, there, seq)] for at, index in table]
        grad = jnp.concatenate(rows, axis=0)
        for n in range(half // LANES):
            part = jnp.dot(
                act,
                grad[:, n * LANES : (n + 1) * LANES],
                preferred_element_type=jnp.float32,
            )
            at = (slice(None), slice(n * LANES, (n + 1) * LANES))
            if not first:
                total[at] += part * part
            elif last:
                total[at] = before[: total.shape[0], at[1]] * back[:, at[1]] + part * part
            elif more == "after":
                total[at] = refs[count][at] + part * part
            else:
                total[at] = part * part

    for source in sources:
        add(source, 0, first=source == sources[0])

    @pl.loop(1, SEQS_DP)
    def _(seq):
        for source in sources:
            add(source, seq)

    if last:
        where = 1 - core[0] if swapped else core[0]
        write_out(total, turned, out, sem, where, seqs)
    elif more != "before":
        peak = jnp.max(total[...], axis=(0, 1), keepdims=True)
        exponent = jnp.floor(jnp.log2(jnp.maximum(peak, jnp.float32(1e-30))))
        sent[: total.shape[0], :] = total[...] * jnp.exp2(SCALE - exponent)
        sent[total.shape[0] :, :] = jnp.broadcast_to(exponent, (ROWS, half))


def add_side(
    seqs, core, acts, grads, table, swapped, before=None, out=None, sources=(0, 1, 2, 3), more=""
):
    acts = [acts[k] for k in sources]
    _, feats, tokens = acts[0].shape
    half = grads[0].shape[-1]
    last = before is not None and more != "after"
    total = jax.ShapeDtypeStruct((feats, half), jnp.float32)
    args = [core, *acts, *grads]
    specs = [pl.BlockSpec(memory_space=pltpu.SMEM)] + [VMEM] * (len(args) - 1)
    anywhere = pl.BlockSpec(memory_space=pl.ANY)
    if last:
        args.append(before)
        specs.append(VMEM)
        if swapped:
            args.append(out)
            specs.append(anywhere)
        result = dict(
            out_shape=jax.ShapeDtypeStruct((2 * half, feats), jnp.float32),
            out_specs=anywhere,
            scratch_shapes=[
                pltpu.VMEM(total.shape, jnp.float32),
                pltpu.VMEM((half, feats), jnp.float32),
                pltpu.SemaphoreType.DMA((PARTS,)),
            ],
            input_output_aliases={len(args) - 1: 0} if swapped else {},
        )
    else:
        if more == "after":
            args.append(before)
            specs.append(VMEM)
        rows = feats + (0 if more == "before" else ROWS)
        result = dict(
            out_shape=jax.ShapeDtypeStruct((rows, half), jnp.float32),
            out_specs=VMEM,
            scratch_shapes=[pltpu.VMEM(total.shape, jnp.float32)],
        )
    return pl.pallas_call(
        functools.partial(square_sum, seqs, table, swapped, last, sources, more, len(grads)),
        in_specs=specs,
        compiler_params=pltpu.CompilerParams(vmem_limit_bytes=6 * 2**20),
        cost_estimate=pl.CostEstimate(
            flops=2 * 3 * len(sources) * tokens * half * feats,
            bytes_accessed=8 * 2**20,
            transcendentals=0,
        ),
        **result,
    )(*args)


def finish_body(seqs, core, given_total, before, token, given, out, turned, sem, total):
    back = jnp.exp2(before[-8:, :][:1] - SCALE)
    total[...] = given_total[...] + before[: total.shape[0], :] * back
    write_out(total, turned, out, sem, 1 - core[0], seqs)


def finish(seqs, core, total, before, token, out):
    feats, half = total.shape
    anywhere = pl.BlockSpec(memory_space=pl.ANY)
    return pl.pallas_call(
        functools.partial(finish_body, seqs),
        in_specs=[pl.BlockSpec(memory_space=pltpu.SMEM), VMEM, VMEM, anywhere, anywhere],
        out_specs=anywhere,
        out_shape=jax.ShapeDtypeStruct(out.shape, jnp.float32),
        scratch_shapes=[
            pltpu.VMEM((half, feats), jnp.float32),
            pltpu.SemaphoreType.DMA((PARTS,)),
            pltpu.VMEM((feats, half), jnp.float32),
        ],
        input_output_aliases={4: 0},
        compiler_params=pltpu.CompilerParams(vmem_limit_bytes=6 * 2**20),
    )(core, total, before, token, out)


def to_owner(grads, core, zlo):
    seq_dev, rows, width = grads.shape
    block = grads.reshape(seq_dev, rows, 2, 4, 2, width // 16).transpose(4, 3, 2, 0, 1, 5)
    mine = lax.dynamic_index_in_dim(block, core, 0, keepdims=False)
    other = lax.dynamic_index_in_dim(block, 1 - core, 0, keepdims=False)
    other = swap(other, "core")
    low = jnp.where(core == 0, mine, other)
    high = jnp.where(core == 0, other, mine)
    both = jnp.concatenate([low, high], axis=3)
    x = lax.axis_index("x")
    way = 1 - 2 * core

    def piece(by):
        return lax.dynamic_index_in_dim(both, (x + by) % 4, 0, keepdims=False)

    parts = [piece(0), send(piece(way), "x", 1), send(piece(-way), "x", -1)]
    parts = jnp.stack([*parts, send(piece(2), "x", 2)])
    return jnp.stack([lax.dynamic_index_in_dim(parts, z, 1, keepdims=False) for z in (1 - zlo, zlo)])


def cross_zlo(total):
    return swap(total.astype(jnp.float16), "zlo")


def per_device(activations, out_grads):
    zlo, y, zhi, core = (lax.axis_index(a) for a in ("zlo", "y", "zhi", "core"))
    seq_dev, rows, width = out_grads.shape
    seqs = seq_dev * 8
    way = 1 - 2 * core
    offsets = (0, -way, way, 2)
    place = [
        ROWS * (((y + dy) % 4) * 4 + (zhi + dz) % 4) for dy in offsets for dz in offsets
    ]
    place = jnp.stack(place).astype(jnp.int32)
    which = jnp.reshape(core, (1,)).astype(jnp.int32)

    g = to_owner(out_grads, core, zlo)
    acts = turn(place, activations)
    g, acts = level((g, acts))

    z1p, z1q = send(g[0], "zhi", 1), send(g[0], "zhi", -1)
    own_p, own_q = send(g, "y", 1), send(g, "y", -1)
    ap = send(acts, "x", 1)
    z1p, z1q, own_p, own_q, ap, g, acts = level((z1p, z1q, own_p, own_q, ap, g, acts))

    z1f = send(z1p, "zhi", 1)
    own_f = send(own_p, "y", 1)
    aq = send(acts, "x", -1)
    z1p, z1q, z1f, own_p, own_q, own_f, g = level(
        (z1p, z1q, z1f, own_p, own_q, own_f, g)
    )

    r1 = jnp.stack([z1p, z1q, z1f])
    y1p, y1q = send(r1, "y", 1), send(r1, "y", -1)
    z2p, z2q = send(g[1], "zhi", 1), send(g[1], "zhi", -1)
    r1, y1p, y1q, z2p, z2q, ap, aq, acts, own_p, own_q = level(
        (r1, y1p, y1q, z2p, z2q, ap, aq, acts, own_p, own_q)
    )

    z2f = send(z2p, "zhi", 1)
    w1p = jnp.concatenate([own_p[:1], y1p])
    y1f = send(y1p, "y", 1)
    af = send(ap, "x", 1)
    some1 = jnp.stack(
        [jnp.concatenate([g[:1], r1]), w1p, jnp.concatenate([own_q[:1], y1q])]
    )
    some1_t = swap(some1, "core")
    w1f = jnp.concatenate([own_f[:1], y1f])

    def whole(at, *index):
        return [(at, (*index, dz)) for dz in range(4)]

    acts = [acts, ap, aq, af]
    table = order([whole(0, 0), whole(0, 1), whole(0, 2), whole(1)], False)
    first = add_side(
        seqs, which, acts, [some1, w1f], table, False, None, None, (0, 1, 2), "before"
    )
    z2p, z2q, z2f, own_p, own_q, some1_t, first, acts = level(
        (z2p, z2q, z2f, own_p, own_q, some1_t, first, acts)
    )

    r2 = jnp.stack([z2p, z2q, z2f])
    y2p, y2q = send(r2, "y", 1), send(r2, "y", -1)
    some2 = jnp.stack([w1f, jnp.concatenate([g[1:], r2])])
    some2_t = swap(some2, "core")

    first = add_side(
        seqs, which, acts, [some1, w1f], table, False, first, None, (3,), "after"
    )
    first = cross_zlo(first)
    table = order([whole(0, 0), whole(0, 1), whole(0, 2), whole(1, 0)], True)
    second = add_side(seqs, which, acts, [some1_t, some2_t], table, True)
    first, second, y2p, y2q, own_p, own_q = level(
        (first, second, y2p, y2q, own_p, own_q)
    )

    y2f = send(y2p, "y", 1)
    second = cross_zlo(second)
    some3 = jnp.concatenate([own_p[1:], y2p, own_q[1:], y2q, own_f[1:]])
    some3_t = swap(some3, "core")
    def last_blocks():
        below = [(1, (dz,)) for dz in range(4)]
        above = [(1, (4 + dz,)) for dz in range(4)]
        return [whole(0, 1), below, above, [(1, (8,))] + [(2, (dz,)) for dz in range(3)]]

    table = order(last_blocks(), False)
    grads = [some2, some3, y2f]
    out = add_side(seqs, which, acts, grads, table, False, first.astype(jnp.float32))
    y2f_t = swap(y2f, "core")
    second, out = level((second, out))
    token = swap(second[-ROWS:, :128].astype(jnp.float32), "core")
    table = order(last_blocks(), True)
    grads = [some2_t, some3_t, y2f_t]
    rest = add_side(seqs, which, acts, grads, table, True, more="before")
    second, token, rest = level((second, token, rest))
    return finish(seqs, which, rest, second.astype(jnp.float32), token, out)


def solution(mesh):
    fine = Mesh(mesh.devices.reshape(SIZES), AXES)
    dp, tensor = AXES[:2], AXES[2:]
    placed = (P(dp, None, tensor), P(dp, tensor, None))
    return jax.shard_map(
        per_device, mesh=fine, in_specs=placed, out_specs=P(dp, tensor), check_vma=False
    )
```
